32 devices in a mesh: row: 4 (over z), col: 8 (over y, x, core).
Axes of the slice: x: 2, y: 2, z: 4, core: 2. Of those that a mesh axis runs over, the one named last changes fastest.
Arguments:
- tokens: bfloat16 [8192, 1024], P(('row', 'col')), may hold values from -6 to 6
- out_grad: bfloat16 [8192, 1024], P(('row', 'col')), may hold values from -6 to 6
- expert_ids: int32 [8192], P(('row', 'col')), may hold values from 0 to 31, as said below
- router_logits: float32 [8192, 32], P(('row', 'col')), may hold values from -6 to 273
- router_weight: bfloat16 [32, 1024], P(('row', 'col')), may hold values from -0.1875 to 0.1875
- w_in: bfloat16 [32, 1024, 2048], P(('row', 'col')), may hold values from -0.1875 to 0.1875
- w_out: bfloat16 [32, 2048, 1024], P(('row', 'col')), may hold values from -0.125 to 0.125
Outputs:
- d_tokens: bfloat16 [8192, 1024], P(('row', 'col'))
- d_w_in: bfloat16 [32, 1024, 2048], P(('row', 'col'))
- d_w_out: bfloat16 [32, 2048, 1024], P(('row', 'col'))
- d_router: float32 [32, 1024], P(('row', 'col'))
The draws below stay inside these ranges and needn't reach their ends.
Inputs may be any that keep to these rules, and one draw needn't show every extreme that they name: `expert_ids`: among the 256 tokens of one device no expert is chosen more than 16 times, and one expert is chosen exactly 16 times by the tokens of every device.
All inputs are finite; a program needn't handle non-finite values.
Results may differ from the reference program's by a relative error of at most 0.017.
Values may be sent and summed in bfloat16 or wider, within the bound.
A program may use at most 128 MiB of HBM per device.

```python
import jax
import jax.numpy as jnp
from jax import lax

D = 1024
F = 2048
TOK_DEV = 256
EXPERTS = 32
CAP = 16
TOKENS = 8192


def route_table(key):
    sources = TOKENS // TOK_DEV
    slots = EXPERTS * CAP
    popular = jax.random.permutation(jax.random.fold_in(key, 11), EXPERTS).astype(jnp.int32)
    slot_expert = jnp.arange(slots, dtype=jnp.int32) // CAP

    def one_source(index):
        source_key = jax.random.fold_in(jax.random.fold_in(key, 12), index)
        noise = jax.random.randint(source_key, (slots,), 0, 1024, dtype=jnp.int32)
        score = noise + popular[slot_expert] * 8
        score = jnp.where(popular[slot_expert] == 0, -1, score) + 1
        order = jnp.argsort(score * slots + jnp.arange(slots, dtype=jnp.int32), stable=True)
        picked = slot_expert[order[:TOK_DEV]]
        shuffle = jax.random.permutation(jax.random.fold_in(source_key, 1), TOK_DEV)
        return picked[shuffle]
    return jax.vmap(one_source)(jnp.arange(sources, dtype=jnp.int32)).reshape(TOKENS).astype(jnp.int32)


def draw_expert_ids(key, part):
    return route_table(key)


def draw_router_logits(key, part):
    chosen_ids = route_table(key)
    key = jax.random.fold_in(key, 5)
    keys = jax.random.split(key, 2)
    base = jnp.clip(1.5 * jax.random.normal(keys[0], (TOKENS, EXPERTS), jnp.float32), -6.0, 6.0)
    columns = jnp.arange(EXPERTS, dtype=jnp.int32)[None, :]
    chosen = (chosen_ids[:, None] == columns).astype(jnp.float32)
    boost = jax.random.uniform(keys[1], (TOKENS, 1), jnp.float32, 3.0, 7.0)
    logits = base + boost * chosen
    return logits.astype(jnp.float32)


def block_scale(own_key, dims, shards, least, top_value):
    level, own = 1.0, jax.random.fold_in(own_key, 6)
    for position, shards_of in shards:
        heights = jnp.exp(jax.random.uniform(jax.random.fold_in(own, position), (shards_of,), jnp.float32, least / len(shards), top_value / len(shards)))
        level = level * jnp.repeat(heights, dims[position] // shards_of).reshape([-1 if axis == position else 1 for axis in range(len(dims))])
    return level


def centred(own_key, extent, scale, bound, cuts=(), held_as=jnp.bfloat16):
    gain = block_scale(own_key, extent, cuts, -0.22, 0.18) if cuts else 1.0
    array = jax.random.normal(own_key, extent, jnp.float32) * scale * gain
    return jnp.minimum(jnp.maximum(array, -bound), bound).astype(held_as)


def setup_inputs(seed: int = 0) -> dict:
    seeds = jax.random.split(jax.random.key(seed), 8)
    return {
        "tokens": centred(seeds[0], (TOKENS, D), 1.0, 6.0, ((0, 32),)),
        "out_grad": centred(seeds[1], (TOKENS, D), 1.0, 6.0, ((0, 32),)),
        "expert_ids": draw_expert_ids(jax.random.fold_in(seeds[7], 71), 0),
        "router_logits": draw_router_logits(jax.random.fold_in(seeds[7], 71), 0),
        "router_weight": centred(seeds[4], (EXPERTS, D), D ** -0.5, 0.1875, ((0, 32),)),
        "w_in": centred(seeds[5], (EXPERTS, D, F), D ** -0.5, 0.1875, ((0, 32),)),
        "w_out": centred(seeds[6], (EXPERTS, F, D), F ** -0.5, 0.125, ((0, 32),)),
    }


def reference(tokens, out_grad, expert_ids, router_logits, router_weight, w_in, w_out):
    sources = TOKENS // TOK_DEV
    slots = EXPERTS * CAP
    grouped = expert_ids.reshape(sources, TOK_DEV).astype(jnp.int32)
    onehot = (grouped[:, :, None] == jnp.arange(EXPERTS, dtype=jnp.int32)[None, None, :]).astype(jnp.int32)
    earlier = jnp.cumsum(onehot, axis=1) - onehot
    ranks = jnp.sum(earlier * onehot, axis=2)
    slot = grouped * CAP + ranks
    flat_slot = (jnp.arange(sources, dtype=jnp.int32)[:, None] * slots + slot).reshape(TOKENS).astype(jnp.int32)
    probs = jax.nn.softmax(router_logits.astype(jnp.float32), axis=-1)
    chosen = (expert_ids[:, None] == jnp.arange(EXPERTS, dtype=jnp.int32)[None, :]).astype(jnp.float32)
    gate = jnp.sum(probs * chosen, axis=1)
    scaled = (gate[:, None] * out_grad.astype(jnp.float32)).astype(jnp.bfloat16)
    routed_all = jnp.zeros((sources * slots, D), jnp.bfloat16).at[flat_slot].set(tokens)
    scaled_all = jnp.zeros((sources * slots, D), jnp.bfloat16).at[flat_slot].set(scaled)
    routed_all = routed_all.reshape(sources, EXPERTS, CAP, D).transpose(1, 0, 2, 3).reshape(EXPERTS, sources * CAP, D)
    scaled_all = scaled_all.reshape(sources, EXPERTS, CAP, D).transpose(1, 0, 2, 3).reshape(EXPERTS, sources * CAP, D)

    def expert(operands):
        routed, scaled_rows, inner_weight, outer_weight = operands
        pre_act = jnp.dot(routed, inner_weight, preferred_element_type=jnp.float32)
        hidden = jnp.maximum(pre_act, 0.0).astype(jnp.bfloat16)
        expert_out = jnp.dot(hidden, outer_weight, preferred_element_type=jnp.float32).astype(jnp.bfloat16)
        back = jnp.dot(scaled_rows, outer_weight.T, preferred_element_type=jnp.float32)
        hidden_grad = jnp.where(pre_act > 0.0, back, 0.0).astype(jnp.bfloat16)
        grad_in = jnp.dot(hidden_grad, inner_weight.T, preferred_element_type=jnp.float32).astype(jnp.bfloat16)
        grad_inner = jnp.dot(routed.T, hidden_grad, preferred_element_type=jnp.float32).astype(jnp.bfloat16)
        grad_outer = jnp.dot(hidden.T, scaled_rows, preferred_element_type=jnp.float32).astype(jnp.bfloat16)
        return grad_in, expert_out, grad_inner, grad_outer

    grad_in, expert_out, d_w_in, d_w_out = lax.map(expert, (routed_all, scaled_all, w_in, w_out))
    grad_in = grad_in.reshape(EXPERTS, sources, CAP, D).transpose(1, 0, 2, 3).reshape(sources * slots, D)
    expert_out = expert_out.reshape(EXPERTS, sources, CAP, D).transpose(1, 0, 2, 3).reshape(sources * slots, D)
    back_in = grad_in[flat_slot]
    back_out = expert_out[flat_slot]
    gate_grad = jnp.sum(out_grad.astype(jnp.float32) * back_out.astype(jnp.float32), axis=1)
    logit_grad = ((gate_grad * gate)[:, None] * (chosen - probs)).astype(jnp.bfloat16)
    d_router = jnp.dot(logit_grad.T, tokens, preferred_element_type=jnp.float32)
    router_part = jnp.dot(logit_grad, router_weight, preferred_element_type=jnp.float32)
    d_tokens = (back_in.astype(jnp.float32) + router_part).astype(jnp.bfloat16)
    return d_tokens, d_w_in, d_w_out, d_router
```

```python
import functools

import jax
import jax.numpy as jnp
from jax import lax
from jax.experimental import pallas as pl
from jax.experimental.pallas import tpu as pltpu
from jax.sharding import PartitionSpec as P

MESH = pl.DeviceIdType.MESH
BF = jnp.bfloat16
F32 = jnp.float32


def dot(a, b, dims=((1,), (0,)), **kw):
    return lax.dot_general(a, b, (dims, ((), ())), preferred_element_type=F32, **kw)


def xor_row(row, dz):
    out, bit = 0, 1
    while bit < 8:
        out = out + bit * (((row // bit) % 2 + (dz // bit) % 2) % 2)
        bit *= 2
    return out


def kernel(
    n_row, n_col, cap, fb,
    tok_ref, og_ref, ids_ref, logit_ref, rw_ref, wi_hbm, wo_hbm,
    dtok_ref, drouter_ref, dwi_hbm, dwo_hbm,
    wi, wo, send_t, send_s, recv_t, recv_s, gout, gback, hid, hgr, acc,
    rwrecv, rwmat, scsend, screcv, scmat, drsend, drrecv,
    wsem, osem, ssem, rt_sem, rs_sem, rg_sem, small_sem,
):
    n = n_row * n_col
    row = lax.axis_index("row")
    col = lax.axis_index("col")
    me = row * n_col + col
    tok, width = tok_ref.shape
    ffn = wi.shape[1]
    crows = n_col * cap
    order = list(range(n_row - 1, -1, -1))

    def rows_of(dev):
        return pl.ds(pl.multiple_of(dev * cap, cap), cap)

    def chunk_of(r):
        return pl.ds(pl.multiple_of(r * crows, crows), crows)

    load_i = pltpu.make_async_copy(wi_hbm.at[0], wi, wsem.at[0])
    load_o = pltpu.make_async_copy(wo_hbm.at[0], wo, wsem.at[1])
    load_i.start()
    load_o.start()

    barrier = pltpu.get_barrier_semaphore()

    def others(body):
        def step(k, c):
            peer = lax.rem(me + k, n)
            body(peer, (peer // n_col, lax.rem(peer, n_col)))
            return c
        lax.fori_loop(1, n, step, 0)

    others(lambda peer, dev: pl.semaphore_signal(
        barrier, inc=1, device_id=dev, device_id_type=MESH))

    ids = ids_ref[...]
    lanes = lax.broadcasted_iota(jnp.int32, (tok, n), 1)
    chosen = (ids == lanes).astype(F32)
    logits = logit_ref[...]
    ex = jnp.exp(logits - jnp.max(logits, axis=1, keepdims=True))
    probs = ex / jnp.sum(ex, axis=1, keepdims=True)
    gate = jnp.sum(probs * chosen, axis=1, keepdims=True)
    it0 = lax.broadcasted_iota(jnp.int32, (tok, tok), 0)
    it1 = lax.broadcasted_iota(jnp.int32, (tok, tok), 1)
    earlier = dot((it1 < it0).astype(F32).astype(BF), chosen.astype(BF))
    rank = jnp.sum(earlier * chosen, axis=1, keepdims=True)
    slot = ids.astype(F32) * cap + rank
    slot_row = jnp.sum(jnp.where(it0 == it1, slot, 0.0), axis=0, keepdims=True)
    tokens = tok_ref[...]
    scaled = (gate * og_ref[...].astype(F32)).astype(BF)

    def fill(r):
        at = lax.broadcasted_iota(jnp.int32, (crows, tok), 0).astype(F32) + (
            r * crows).astype(F32)
        pick = (at == slot_row).astype(F32).astype(BF)
        send_t[chunk_of(r), :] = dot(pick, tokens).astype(BF)
        send_s[chunk_of(r), :] = dot(pick, scaled).astype(BF)

    def push(src, dst, sem, rsem, dev):
        pltpu.make_async_remote_copy(
            src_ref=src, dst_ref=dst, send_sem=sem, recv_sem=rsem,
            device_id=dev, device_id_type=MESH,
        ).start()

    def dispatch(dz, j):
        r = xor_row(row, dz)
        c = lax.rem(col + j, n_col)
        peer = r * n_col + c
        push(send_t.at[rows_of(peer)], recv_t.at[rows_of(me)], ssem.at[0], rt_sem.at[dz], (r, c))
        push(send_s.at[rows_of(peer)], recv_s.at[rows_of(me)], ssem.at[1], rs_sem.at[dz], (r, c))

    def col_loop(first, body):
        def step(j, c):
            body(j)
            return c
        lax.fori_loop(first, n_col, step, 0)

    half = n_row // 2
    phases = [(half, 0)] + [(half + i, i) for i in range(1, half)]
    first = True
    for far, near in phases:
        fill(xor_row(row, far))
        fill(xor_row(row, near))
        if first:
            pl.semaphore_wait(barrier, n - 1)
            first = False
        dispatch(far, 0)
        if near == 0:
            pltpu.make_async_copy(
                send_t.at[rows_of(me)], recv_t.at[rows_of(me)], rt_sem.at[0]).start()
            pltpu.make_async_copy(
                send_s.at[rows_of(me)], recv_s.at[rows_of(me)], rs_sem.at[0]).start()
        else:
            dispatch(near, 0)

        def both(j, far=far, near=near):
            dispatch(far, j)
            dispatch(near, j)
        col_loop(1, both)

    rwrecv[pl.ds(me, 1)] = rw_ref[...].astype(F32)[None]
    others(lambda peer, dev: push(
        rwrecv.at[me], rwrecv.at[me], ssem.at[3], small_sem.at[0], dev))

    load_i.wait()
    load_o.wait()

    def wait_rows(ref, sl, sem):
        pltpu.make_async_copy(ref.at[sl], ref.at[sl], sem).wait()

    eye = (lax.broadcasted_iota(jnp.int32, (crows, crows), 0)
           == lax.broadcasted_iota(jnp.int32, (crows, crows), 1))

    for near, far in [(b, a) for a, b in phases]:
        for dz in (near, far):
            r = xor_row(row, dz)
            sl = chunk_of(r)
            wait_rows(recv_t, sl, rt_sem.at[dz])
            wait_rows(recv_s, sl, rs_sem.at[dz])
            acc[...] = jnp.zeros_like(acc)

            def block(f, v, sl=sl):
                fs = pl.ds(pl.multiple_of(f * fb, fb), fb)
                w1 = wi[:, fs]
                pre = dot(recv_t[sl, :], w1)
                back = dot(recv_s[sl, :], wo[fs, :], ((1,), (1,)))
                h = jnp.maximum(pre, 0.0).astype(BF)
                g = jnp.where(pre > 0.0, back, 0.0).astype(BF)
                hid[sl, fs] = h
                hgr[sl, fs] = g
                acc[...] += dot(g, w1, ((1,), (1,)))
                return v + jnp.sum(h.astype(F32) * back, axis=1, keepdims=True)

            v = lax.fori_loop(0, ffn // fb, block, jnp.zeros((crows, 1), F32))
            gout[sl, :] = acc[...].astype(BF)
            scsend[pl.ds(r, 1)] = jnp.sum(
                jnp.where(eye, v, 0.0), axis=0, keepdims=True)[None]

            def give(j, r=r, dz=dz):
                c = lax.rem(col + j, n_col)
                peer = r * n_col + c
                push(scsend.at[r], screcv.at[me], ssem.at[4], small_sem.at[1], (r, c))
                push(gout.at[rows_of(peer)], gback.at[rows_of(me)], ssem.at[2], rg_sem.at[dz], (r, c))
            if dz == 0:
                pltpu.make_async_copy(
                    gout.at[rows_of(me)], gback.at[rows_of(me)], rg_sem.at[0]).start()
                pltpu.make_async_copy(
                    scsend.at[r], screcv.at[me], small_sem.at[1]).start()
                col_loop(1, give)
            else:
                col_loop(0, give)

    db = min(256, width)

    def grad_in_w(i, c):
        ds = pl.ds(pl.multiple_of(i * db, db), db)
        wi[ds, :] = dot(recv_t[:, ds], hgr[...], ((0,), (0,))).astype(BF)
        pltpu.make_async_copy(wi.at[ds], dwi_hbm.at[0, ds], osem.at[0]).start()
        return c
    lax.fori_loop(0, width // db, grad_in_w, 0)

    def grad_out_w(i, c):
        fs = pl.ds(pl.multiple_of(i * fb, fb), fb)
        wo[fs, :] = dot(hid[:, fs], recv_s[...], ((0,), (0,))).astype(BF)
        pltpu.make_async_copy(wo.at[fs], dwo_hbm.at[0, fs], osem.at[1]).start()
        return c
    lax.fori_loop(0, ffn // fb, grad_out_w, 0)

    pltpu.make_async_copy(screcv, screcv, small_sem.at[1]).wait()
    for e in range(n):
        scmat[e:e + 1, :] = screcv[e]
    picked = dot(chosen, scmat[...], precision=lax.Precision.HIGHEST)
    lane = lax.broadcasted_iota(jnp.int32, (tok, crows), 1).astype(F32)
    mine = (col * cap).astype(F32) + rank
    vg = jnp.sum(jnp.where(lane == mine, picked, 0.0), axis=1, keepdims=True)
    lg = (vg * (chosen - probs)).astype(BF)
    part = dot(lg, tokens, ((0,), (0,)))
    for e in range(n):
        drsend[e] = part[e:e + 1, :]
    others(lambda peer, dev: push(
        drsend.at[peer], drrecv.at[me], ssem.at[5], small_sem.at[2], dev))
    drrecv[pl.ds(me, 1)] = drsend[pl.ds(me, 1)]

    wait_rows(rwrecv, pl.ds(0, n - 1), small_sem.at[0])
    for e in range(n):
        rwmat[e:e + 1, :] = rwrecv[e]
    router_part = dot(lg, rwmat[...].astype(BF))
    for dz in order[::-1]:
        wait_rows(gback, chunk_of(xor_row(row, dz)), rg_sem.at[dz])
    at = lax.broadcasted_iota(jnp.int32, (tok, n * cap), 1).astype(F32)
    pick = (at == slot).astype(F32).astype(BF)
    dtok_ref[...] = (dot(pick, gback[...]) + router_part).astype(BF)

    wait_rows(drrecv, pl.ds(0, n - 1), small_sem.at[2])
    drouter_ref[...] = jnp.sum(drrecv[...], axis=0)

    most = pl.ds(0, (n - 1) * cap)
    wait_rows(send_t, most, ssem.at[0])
    wait_rows(send_s, most, ssem.at[1])
    wait_rows(gout, most, ssem.at[2])
    wait_rows(rwrecv, pl.ds(0, n - 1), ssem.at[3])
    wait_rows(screcv, pl.ds(0, n - 1), ssem.at[4])
    wait_rows(drsend, pl.ds(0, n - 1), ssem.at[5])
    pltpu.make_async_copy(wi, dwi_hbm.at[0], osem.at[0]).wait()
    pltpu.make_async_copy(wo, dwo_hbm.at[0], osem.at[1]).wait()


def per_device(tokens, out_grad, expert_ids, router_logits, router_weight, w_in, w_out):
    n_row = lax.axis_size("row")
    n_col = lax.axis_size("col")
    n = n_row * n_col
    tok, width = tokens.shape
    ffn = w_in.shape[2]
    cap = max(16, 2 * tok // n)
    rows = n * cap
    crows = n_col * cap
    vm = pl.BlockSpec(memory_space=pltpu.VMEM)
    hbm = pl.BlockSpec(memory_space=pl.ANY)
    dma = pltpu.SemaphoreType.DMA
    big = pltpu.VMEM((rows, width), BF)
    d_tokens, d_router, d_wi, d_wo = pl.pallas_call(
        functools.partial(kernel, n_row, n_col, cap, min(512, ffn)),
        out_shape=(
            jax.ShapeDtypeStruct((tok, width), BF),
            jax.ShapeDtypeStruct((1, width), F32),
            jax.ShapeDtypeStruct(w_in.shape, BF),
            jax.ShapeDtypeStruct(w_out.shape, BF),
        ),
        in_specs=[vm] * 5 + [hbm] * 2,
        out_specs=(vm, vm, hbm, hbm),
        scratch_shapes=[
            pltpu.VMEM((width, ffn), BF),
            pltpu.VMEM((ffn, width), BF),
            big, big, big, big, big, big,
            pltpu.VMEM((rows, ffn), BF),
            pltpu.VMEM((rows, ffn), BF),
            pltpu.VMEM((crows, width), F32),
            pltpu.VMEM((n, 1, width), F32),
            pltpu.VMEM((n, width), F32),
            pltpu.VMEM((n_row, 1, crows), F32),
            pltpu.VMEM((n, 1, crows), F32),
            pltpu.VMEM((n, crows), F32),
            pltpu.VMEM((n, 1, width), F32),
            pltpu.VMEM((n, 1, width), F32),
            dma((2,)),
            dma((2,)),
            dma((6,)),
            dma((n_row,)),
            dma((n_row,)),
            dma((n_row,)),
            dma((3,)),
        ],
        compiler_params=pltpu.CompilerParams(
            collective_id=0, has_side_effects=True, vmem_limit_bytes=60 * 1024 * 1024
        ),
        cost_estimate=pl.CostEstimate(
            flops=10 * rows * width * ffn, bytes_accessed=8 * width * ffn, transcendentals=0
        ),
    )(tokens, out_grad, expert_ids[:, None], router_logits, router_weight, w_in, w_out)
    return d_tokens, d_wi, d_wo, d_router


def solution(mesh):
    both = ("row", "col")
    flat, cube = P(both, None), P(both, None, None)
    return jax.shard_map(
        per_device,
        mesh=mesh,
        in_specs=(flat, flat, P(both), flat, flat, cube, cube),
        out_specs=(flat, cube, cube, flat),
        check_vma=False,
    )
```

```python
import functools

import jax
import jax.numpy as jnp
from jax import lax
from jax.experimental import pallas as pl
from jax.experimental.pallas import tpu as pltpu
from jax.sharding import PartitionSpec as P

MESH = pl.DeviceIdType.MESH
BF = jnp.bfloat16
F32 = jnp.float32


def dot(a, b, dims=((1,), (0,)), **kw):
    return lax.dot_general(a, b, (dims, ((), ())), preferred_element_type=F32, **kw)


def xor_row(row, dz):
    out, bit = 0, 1
    while bit < 8:
        out = out + bit * (((row // bit) % 2 + (dz // bit) % 2) % 2)
        bit *= 2
    return out


def kernel(
    n_row, n_col, cap, fb,
    tok_ref, og_ref, ids_ref, logit_ref, rw_ref, wi_hbm, wo_hbm,
    dtok_ref, drouter_ref, routed_hbm, scaled_hbm, hid_hbm, hgr_hbm,
    wi, wo, send_t, send_s, recv_t, recv_s, gout, gback, hid, hgr, acc,
    rwrecv, rwmat, scsend, screcv, scmat, drsend, drrecv, drsum, drz,
    wsem, osem, ssem, rt_sem, rs_sem, rg_sem, small_sem,
):
    n = n_row * n_col
    row = lax.axis_index("row")
    col = lax.axis_index("col")
    me = row * n_col + col
    tok, width = tok_ref.shape
    ffn = wi.shape[1]
    crows = n_col * cap

    def rows_of(dev):
        return pl.ds(pl.multiple_of(dev * cap, cap), cap)

    def chunk_of(r):
        return pl.ds(pl.multiple_of(r * crows, crows), crows)

    def rows_at(c):
        return pl.ds(c * n_row, n_row)

    load_i = pltpu.make_async_copy(wi_hbm.at[0], wi, wsem.at[0])
    load_o = pltpu.make_async_copy(wo_hbm.at[0], wo, wsem.at[1])
    load_i.start()
    load_o.start()

    barrier = pltpu.get_barrier_semaphore()

    def greet(k, c):
        peer = lax.rem(me + k, n)
        pl.semaphore_signal(
            barrier, inc=1, device_id=(peer // n_col, lax.rem(peer, n_col)),
            device_id_type=MESH)
        return c
    lax.fori_loop(1, n, greet, 0)

    ids = ids_ref[...]
    chosen = (ids == lax.broadcasted_iota(jnp.int32, (n, tok), 0)).astype(F32)
    logits = logit_ref[...]
    ex = jnp.exp(logits - jnp.max(logits, axis=0, keepdims=True))
    probs = ex / jnp.sum(ex, axis=0, keepdims=True)
    gate = jnp.sum(probs * chosen, axis=0, keepdims=True)
    it0 = lax.broadcasted_iota(jnp.int32, (tok, tok), 0)
    it1 = lax.broadcasted_iota(jnp.int32, (tok, tok), 1)
    earlier = dot(chosen.astype(BF), (it0 < it1).astype(F32).astype(BF))
    rank = jnp.sum(earlier * chosen, axis=0, keepdims=True)
    slot = ids.astype(F32) * cap + rank

    def upright(x):
        return jnp.sum(jnp.where(it0 == it1, x, 0.0), axis=1, keepdims=True)

    tokens = tok_ref[...]
    scaled = (upright(gate) * og_ref[...].astype(F32)).astype(BF)

    def fill(r):
        at = lax.broadcasted_iota(jnp.int32, (crows, tok), 0).astype(F32) + (
            r * crows).astype(F32)
        pick = (at == slot).astype(F32).astype(BF)
        send_t[chunk_of(r), :] = dot(pick, tokens).astype(BF)
        send_s[chunk_of(r), :] = dot(pick, scaled).astype(BF)

    def push(src, dst, sem, rsem, dev):
        pltpu.make_async_remote_copy(
            src_ref=src, dst_ref=dst, send_sem=sem, recv_sem=rsem,
            device_id=dev, device_id_type=MESH,
        ).start()

    def col_loop(first, last, body):
        def step(j, c):
            body(lax.rem(col + j, n_col))
            return c
        lax.fori_loop(first, last, step, 0)

    def dispatch(dz):
        r = xor_row(row, dz)

        def send(c):
            peer = rows_of(r * n_col + c)
            push(send_t.at[peer], recv_t.at[rows_of(me)], ssem.at[0], rt_sem.at[dz], (r, c))
            push(send_s.at[peer], recv_s.at[rows_of(me)], ssem.at[1], rs_sem.at[dz], (r, c))
        col_loop(0 if dz else 1, n_col, send)

    half = n_row // 2
    near, far = list(range(half)), list(range(half, n_row))
    for dz in far[:1] + near + far[1:]:
        fill(xor_row(row, dz))
        if dz == far[0]:
            pl.semaphore_wait(barrier, n - 1)
        if dz == 0:
            pltpu.make_async_copy(
                send_t.at[rows_of(me)], recv_t.at[rows_of(me)], rt_sem.at[0]).start()
            pltpu.make_async_copy(
                send_s.at[rows_of(me)], recv_s.at[rows_of(me)], rs_sem.at[0]).start()
        dispatch(dz)

    mine = col * n_row + row
    rwrecv[pl.ds(mine, 1)] = rw_ref[...].astype(F32)[None]
    for k in range(1, n_row):
        push(rwrecv.at[mine], rwrecv.at[mine], ssem.at[3], small_sem.at[0],
             (lax.rem(row + k, n_row), col))

    def wait_rows(ref, sl, sem):
        pltpu.make_async_copy(ref.at[sl], ref.at[sl], sem).wait()

    load_i.wait()
    load_o.wait()
    eye = (lax.broadcasted_iota(jnp.int32, (crows, crows), 0)
           == lax.broadcasted_iota(jnp.int32, (crows, crows), 1))

    def give(dz, first, last):
        r = xor_row(row, dz)

        def send(c):
            push(gout.at[rows_of(r * n_col + c)], gback.at[rows_of(me)],
                 ssem.at[2], rg_sem.at[dz], (r, c))
        col_loop(first, last, send)

    held = []
    for dz in near + far:
        r = xor_row(row, dz)
        sl = chunk_of(r)
        wait_rows(recv_t, sl, rt_sem.at[dz])
        wait_rows(recv_s, sl, rs_sem.at[dz])
        if dz == far[-1]:
            for before in held:
                give(before, n_col // 2, n_col)
        acc[...] = jnp.zeros_like(acc)

        def block(f, v, sl=sl):
            fs = pl.ds(pl.multiple_of(f * fb, fb), fb)
            w1 = wi[:, fs]
            pre = dot(recv_t[sl, :], w1)
            back = dot(recv_s[sl, :], wo[fs, :], ((1,), (1,)))
            h = jnp.maximum(pre, 0.0).astype(BF)
            g = jnp.where(pre > 0.0, back, 0.0).astype(BF)
            hid[sl, fs] = h
            hgr[sl, fs] = g
            acc[...] += dot(g, w1, ((1,), (1,)))
            return v + jnp.sum(h.astype(F32) * back, axis=1, keepdims=True)

        v = lax.fori_loop(0, ffn // fb, block, jnp.zeros((crows, 1), F32))
        gout[sl, :] = acc[...].astype(BF)
        scsend[pl.ds(r, 1)] = jnp.sum(
            jnp.where(eye, v, 0.0), axis=0, keepdims=True)[None]

        def tell(c, r=r):
            push(scsend.at[r], screcv.at[me], ssem.at[4], small_sem.at[1], (r, c))
        if dz == 0:
            pltpu.make_async_copy(
                gout.at[rows_of(me)], gback.at[rows_of(me)], rg_sem.at[0]).start()
            pltpu.make_async_copy(scsend.at[r], screcv.at[me], small_sem.at[1]).start()
        col_loop(0 if dz else 1, n_col, tell)
        if dz in far[:-1]:
            give(dz, 0, n_col // 2)
            held.append(dz)
        else:
            give(dz, 0 if dz else 1, n_col)
        if dz == 0:
            wait_rows(rwrecv, pl.ds(0, n_row - 1), small_sem.at[0])

            def pass_on(c):
                push(rwrecv.at[rows_at(col)], rwrecv.at[rows_at(col)],
                     ssem.at[6], small_sem.at[3], (row, c))
            col_loop(1, n_col, pass_on)
        for k, (src, dst) in enumerate((
                (recv_t, routed_hbm), (recv_s, scaled_hbm), (hid, hid_hbm), (hgr, hgr_hbm))):
            pltpu.make_async_copy(src.at[sl], dst.at[sl], osem.at[k]).start()

    pltpu.make_async_copy(screcv, screcv, small_sem.at[1]).wait()
    for e in range(n):
        scmat[e:e + 1, :] = screcv[e]
    picked = dot(scmat[...], chosen, ((0,), (0,)), precision=lax.Precision.HIGHEST)
    lane = lax.broadcasted_iota(jnp.int32, (crows, tok), 0).astype(F32)
    own = (col * cap).astype(F32) + rank
    vg = jnp.sum(jnp.where(lane == own, picked, 0.0), axis=0, keepdims=True)
    lg = (vg * (chosen - probs)).astype(BF)
    part = dot(lg, tokens)
    for e in range(n):
        drsend[(e % n_col) * n_row + e // n_col] = part[e:e + 1, :]

    def gather_part(c):
        push(drsend.at[rows_at(c)], drrecv.at[rows_at(col)],
             ssem.at[5], small_sem.at[2], (row, c))
    col_loop(1, n_col, gather_part)
    drrecv[rows_at(col)] = drsend[rows_at(col)]

    others = pl.ds(0, n - n_row)
    wait_rows(rwrecv, others, small_sem.at[3])
    for e in range(n):
        rwmat[e:e + 1, :] = rwrecv[(e % n_col) * n_row + e // n_col]
    router_part = dot(lg, rwmat[...].astype(BF), ((0,), (0,)))

    wait_rows(drrecv, others, small_sem.at[2])
    total = drrecv[0:n_row]
    for c in range(1, n_col):
        total = total + drrecv[c * n_row:(c + 1) * n_row]
    drsum[...] = total
    for k in range(1, n_row):
        r = lax.rem(row + k, n_row)
        push(drsum.at[r], drz.at[row], ssem.at[7], small_sem.at[4], (r, col))
    drz[pl.ds(row, 1)] = drsum[pl.ds(row, 1)]

    at = lax.broadcasted_iota(jnp.int32, (tok, n * cap), 1).astype(F32)
    pick = (at == upright(slot)).astype(F32).astype(BF)
    for dz in near + far:
        wait_rows(gback, chunk_of(xor_row(row, dz)), rg_sem.at[dz])
    dtok_ref[...] = (dot(pick, gback[...]) + router_part).astype(BF)

    wait_rows(drz, pl.ds(0, n_row - 1), small_sem.at[4])
    drouter_ref[...] = jnp.sum(drz[...], axis=0)

    most = pl.ds(0, (n - 1) * cap)
    wait_rows(send_t, most, ssem.at[0])
    wait_rows(send_s, most, ssem.at[1])
    wait_rows(gout, most, ssem.at[2])
    wait_rows(rwrecv, pl.ds(0, n_row - 1), ssem.at[3])
    wait_rows(screcv, pl.ds(0, n - 1), ssem.at[4])
    wait_rows(drsend, others, ssem.at[5])
    wait_rows(rwrecv, others, ssem.at[6])
    wait_rows(drsum, pl.ds(0, n_row - 1), ssem.at[7])
    for k, (src, dst) in enumerate((
            (recv_t, routed_hbm), (recv_s, scaled_hbm), (hid, hid_hbm), (hgr, hgr_hbm))):
        pltpu.make_async_copy(src, dst, osem.at[k]).wait()


def weight_grads(routed, scaled, hid, hgr, dtok, drouter, dwi, dwo, dtok_out, drouter_out):
    dwi[0] = dot(routed[...], hgr[...], ((0,), (0,))).astype(BF)
    dwo[0] = dot(hid[...], scaled[...], ((0,), (0,))).astype(BF)
    dtok_out[...] = dtok[...]
    drouter_out[...] = drouter[...]


def per_device(tokens, out_grad, expert_ids, router_logits, router_weight, w_in, w_out):
    n_row = lax.axis_size("row")
    n_col = lax.axis_size("col")
    n = n_row * n_col
    tok, width = tokens.shape
    ffn = w_in.shape[2]
    cap = max(16, 2 * tok // n)
    rows = n * cap
    crows = n_col * cap
    vm = pl.BlockSpec(memory_space=pltpu.VMEM)
    hbm = pl.BlockSpec(memory_space=pl.ANY)
    dma = pltpu.SemaphoreType.DMA
    big = pltpu.VMEM((rows, width), BF)
    line = pltpu.VMEM((n, 1, width), F32)
    few = pltpu.VMEM((n_row, 1, width), F32)
    limit = 60 * 1024 * 1024
    shape = jax.ShapeDtypeStruct
    d_tokens, d_router, routed, scaled, hid, hgr = pl.pallas_call(
        functools.partial(kernel, n_row, n_col, cap, min(512, ffn)),
        out_shape=(
            shape((tok, width), BF),
            shape((1, width), F32),
            shape((rows, width), BF),
            shape((rows, width), BF),
            shape((rows, ffn), BF),
            shape((rows, ffn), BF),
        ),
        in_specs=[vm] * 5 + [hbm] * 2,
        out_specs=(vm, vm, hbm, hbm, hbm, hbm),
        scratch_shapes=[
            pltpu.VMEM((width, ffn), BF),
            pltpu.VMEM((ffn, width), BF),
            big, big, big, big, big, big,
            pltpu.VMEM((rows, ffn), BF),
            pltpu.VMEM((rows, ffn), BF),
            pltpu.VMEM((crows, width), F32),
            line,
            pltpu.VMEM((n, width), F32),
            pltpu.VMEM((n_row, 1, crows), F32),
            pltpu.VMEM((n, 1, crows), F32),
            pltpu.VMEM((n, crows), F32),
            line, line, few, few,
            dma((2,)),
            dma((4,)),
            dma((8,)),
            dma((n_row,)),
            dma((n_row,)),
            dma((n_row,)),
            dma((5,)),
        ],
        compiler_params=pltpu.CompilerParams(
            collective_id=0, has_side_effects=True, vmem_limit_bytes=limit
        ),
        cost_estimate=pl.CostEstimate(
            flops=6 * rows * width * ffn, bytes_accessed=8 * width * ffn, transcendentals=0
        ),
    )(tokens, out_grad, expert_ids[None, :], router_logits.T, router_weight, w_in, w_out)

    steps = 4
    d_wi, d_wo, d_tokens, d_router = pl.pallas_call(
        weight_grads,
        grid=(steps,),
        out_shape=(
            shape(w_in.shape, BF),
            shape(w_out.shape, BF),
            shape((tok, width), BF),
            shape((1, width), F32),
        ),
        in_specs=[
            pl.BlockSpec((rows, width // steps), lambda i: (0, i)),
            pl.BlockSpec((rows, width), lambda i: (0, 0)),
            pl.BlockSpec((rows, ffn // steps), lambda i: (0, i)),
            pl.BlockSpec((rows, ffn), lambda i: (0, 0)),
            pl.BlockSpec((tok // steps, width), lambda i: (i, 0)),
            pl.BlockSpec((1, width), lambda i: (0, 0)),
        ],
        out_specs=(
            pl.BlockSpec((1, width // steps, ffn), lambda i: (0, i, 0)),
            pl.BlockSpec((1, ffn // steps, width), lambda i: (0, i, 0)),
            pl.BlockSpec((tok // steps, width), lambda i: (i, 0)),
            pl.BlockSpec((1, width), lambda i: (0, 0)),
        ),
        compiler_params=pltpu.CompilerParams(vmem_limit_bytes=limit),
        cost_estimate=pl.CostEstimate(
            flops=4 * rows * width * ffn, bytes_accessed=6 * width * ffn, transcendentals=0
        ),
    )(routed, scaled, hid, hgr, d_tokens, d_router)
    return d_tokens, d_wi, d_wo, d_router


def solution(mesh):
    both = ("row", "col")
    flat, cube = P(both, None), P(both, None, None)
    return jax.shard_map(
        per_device,
        mesh=mesh,
        in_specs=(flat, flat, P(both), flat, flat, cube, cube),
        out_specs=(flat, cube, cube, flat),
        check_vma=False,
    )
```

```python
import functools

import jax
import jax.numpy as jnp
from jax import lax
from jax.experimental import pallas as pl
from jax.experimental.pallas import tpu as pltpu
from jax.sharding import PartitionSpec as P

MESH = pl.DeviceIdType.MESH
BF = jnp.bfloat16
F32 = jnp.float32


def dot(a, b, dims=((1,), (0,)), **kw):
    return lax.dot_general(a, b, (dims, ((), ())), preferred_element_type=F32, **kw)


def xor_row(row, dz):
    out, bit = 0, 1
    while bit < 8:
        out = out + bit * (((row // bit) % 2 + (dz // bit) % 2) % 2)
        bit *= 2
    return out


def kernel(
    n_row, n_col, cap, fb,
    tok_ref, og_ref, ids_ref, logit_ref, rw_ref, wi_hbm, wo_hbm,
    dtok_ref, drouter_ref, dwi_hbm, dwo_hbm,
    wi, wo, send_t, send_s, recv_t, recv_s, gout, gback, hid, hgr, acc,
    rwrecv, rwmat, scsend, screcv, scmat, drsend, drrecv, drsum, drz,
    wsem, osem, ssem, rt_sem, rs_sem, rg_sem, small_sem,
):
    n = n_row * n_col
    row = lax.axis_index("row")
    col = lax.axis_index("col")
    me = row * n_col + col
    tok, width = tok_ref.shape
    ffn = wi.shape[1]
    crows = n_col * cap

    def rows_of(dev):
        return pl.ds(pl.multiple_of(dev * cap, cap), cap)

    def chunk_of(r):
        return pl.ds(pl.multiple_of(r * crows, crows), crows)

    def rows_at(c):
        return pl.ds(c * n_row, n_row)

    load_i = pltpu.make_async_copy(wi_hbm.at[0], wi, wsem.at[0])
    load_o = pltpu.make_async_copy(wo_hbm.at[0], wo, wsem.at[1])
    load_i.start()
    load_o.start()

    barrier = pltpu.get_barrier_semaphore()

    def greet(k, c):
        peer = lax.rem(me + k, n)
        pl.semaphore_signal(
            barrier, inc=1, device_id=(peer // n_col, lax.rem(peer, n_col)),
            device_id_type=MESH)
        return c
    lax.fori_loop(1, n, greet, 0)

    ids = ids_ref[...]
    chosen = (ids == lax.broadcasted_iota(jnp.int32, (n, tok), 0)).astype(F32)
    it0 = lax.broadcasted_iota(jnp.int32, (tok, tok), 0)
    it1 = lax.broadcasted_iota(jnp.int32, (tok, tok), 1)
    earlier = dot(chosen.astype(BF), (it0 < it1).astype(F32).astype(BF))
    rank = jnp.sum(earlier * chosen, axis=0, keepdims=True)
    slot = ids.astype(F32) * cap + rank
    tokens = tok_ref[...]

    def upright(x):
        return jnp.sum(jnp.where(it0 == it1, x, 0.0), axis=1, keepdims=True)

    def fill(ref, values, dz):
        r = xor_row(row, dz)
        at = lax.broadcasted_iota(jnp.int32, (crows, tok), 0).astype(F32) + (
            r * crows).astype(F32)
        pick = (at == slot).astype(F32).astype(BF)
        ref[chunk_of(r), :] = dot(pick, values).astype(BF)

    def push(src, dst, sem, rsem, dev):
        pltpu.make_async_remote_copy(
            src_ref=src, dst_ref=dst, send_sem=sem, recv_sem=rsem,
            device_id=dev, device_id_type=MESH,
        ).start()

    def col_loop(first, last, body):
        def step(j, c):
            body(lax.rem(col + j, n_col))
            return c
        lax.fori_loop(first, last, step, 0)

    def send_tokens(dz, c):
        r = xor_row(row, dz)
        push(send_t.at[rows_of(r * n_col + c)], recv_t.at[rows_of(me)],
             ssem.at[0], rt_sem.at[dz], (r, c))

    def send_scaled(dz, c):
        r = xor_row(row, dz)
        push(send_s.at[rows_of(r * n_col + c)], recv_s.at[rows_of(me)],
             ssem.at[1], rs_sem.at[dz], (r, c))

    def dispatch(far, near, sends):
        for send in sends:
            send(far, col)
            if near:
                send(near, col)

        def both(c):
            for send in sends:
                send(far, c)
                send(near, c)
        col_loop(1, n_col, both)

    half = n_row // 2
    fill(send_t, tokens, half)
    fill(send_t, tokens, 0)
    pl.semaphore_wait(barrier, n - 1)

    mine = col * n_row + row
    rwrecv[pl.ds(mine, 1)] = rw_ref[...].astype(F32)[None]
    for k in range(1, n_row):
        push(rwrecv.at[mine], rwrecv.at[mine], ssem.at[3], small_sem.at[0],
             (lax.rem(row + k, n_row), col))

    dispatch(half, 0, (send_tokens,))
    pltpu.make_async_copy(
        send_t.at[rows_of(me)], recv_t.at[rows_of(me)], rt_sem.at[0]).start()

    logits = logit_ref[...]
    ex = jnp.exp(logits - jnp.max(logits, axis=0, keepdims=True))
    probs = ex / jnp.sum(ex, axis=0, keepdims=True)
    gate = jnp.sum(probs * chosen, axis=0, keepdims=True)
    scaled = (upright(gate) * og_ref[...].astype(F32)).astype(BF)
    fill(send_s, scaled, half)
    fill(send_s, scaled, 0)
    dispatch(half, 0, (send_scaled,))
    pltpu.make_async_copy(
        send_s.at[rows_of(me)], recv_s.at[rows_of(me)], rs_sem.at[0]).start()
    for near in range(1, half):
        for dz in (half + near, near):
            fill(send_t, tokens, dz)
            fill(send_s, scaled, dz)
        dispatch(half + near, near, (send_tokens, send_scaled))

    def wait_rows(ref, sl, sem):
        pltpu.make_async_copy(ref.at[sl], ref.at[sl], sem).wait()

    load_i.wait()
    load_o.wait()
    eye = (lax.broadcasted_iota(jnp.int32, (crows, crows), 0)
           == lax.broadcasted_iota(jnp.int32, (crows, crows), 1))

    def give(dz, first, last):
        r = xor_row(row, dz)

        def send(c):
            push(gout.at[rows_of(r * n_col + c)], gback.at[rows_of(me)],
                 ssem.at[2], rg_sem.at[dz], (r, c))
        col_loop(first, last, send)

    turns = [dz for near in range(half) for dz in (near, half + near)]
    for dz in turns:
        r = xor_row(row, dz)
        sl = chunk_of(r)
        wait_rows(recv_t, sl, rt_sem.at[dz])
        wait_rows(recv_s, sl, rs_sem.at[dz])
        acc[...] = jnp.zeros_like(acc)

        def block(f, v, sl=sl):
            fs = pl.ds(pl.multiple_of(f * fb, fb), fb)
            w1 = wi[:, fs]
            pre = dot(recv_t[sl, :], w1)
            back = dot(recv_s[sl, :], wo[fs, :], ((1,), (1,)))
            h = jnp.maximum(pre, 0.0).astype(BF)
            g = jnp.where(pre > 0.0, back, 0.0).astype(BF)
            hid[sl, fs] = h
            hgr[sl, fs] = g
            acc[...] += dot(g, w1, ((1,), (1,)))
            return v + jnp.sum(h.astype(F32) * back, axis=1, keepdims=True)

        v = lax.fori_loop(0, ffn // fb, block, jnp.zeros((crows, 1), F32))
        gout[sl, :] = acc[...].astype(BF)
        scsend[pl.ds(r, 1)] = jnp.sum(
            jnp.where(eye, v, 0.0), axis=0, keepdims=True)[None]

        def tell(c, r=r):
            push(scsend.at[r], screcv.at[me], ssem.at[4], small_sem.at[1], (r, c))
        if dz == 0:
            pltpu.make_async_copy(
                gout.at[rows_of(me)], gback.at[rows_of(me)], rg_sem.at[0]).start()
            pltpu.make_async_copy(scsend.at[r], screcv.at[me], small_sem.at[1]).start()
        col_loop(0 if dz else 1, n_col, tell)
        give(dz, 0 if dz else 1, n_col)
        if dz == half:
            wait_rows(rwrecv, pl.ds(0, n_row - 1), small_sem.at[0])

            def pass_on(c):
                push(rwrecv.at[rows_at(col)], rwrecv.at[rows_at(col)],
                     ssem.at[6], small_sem.at[3], (row, c))
            col_loop(1, n_col, pass_on)

    pltpu.make_async_copy(screcv, screcv, small_sem.at[1]).wait()
    for e in range(n):
        scmat[e:e + 1, :] = screcv[e]
    picked = dot(scmat[...], chosen, ((0,), (0,)), precision=lax.Precision.HIGHEST)
    lane = lax.broadcasted_iota(jnp.int32, (crows, tok), 0).astype(F32)
    own = (col * cap).astype(F32) + rank
    vg = jnp.sum(jnp.where(lane == own, picked, 0.0), axis=0, keepdims=True)
    lg = (vg * (chosen - probs)).astype(BF)
    part = dot(lg, tokens)
    for e in range(n):
        drsend[(e % n_col) * n_row + e // n_col] = part[e:e + 1, :]

    def gather_part(c):
        push(drsend.at[rows_at(c)], drrecv.at[rows_at(col)],
             ssem.at[5], small_sem.at[2], (row, c))
    col_loop(1, n_col, gather_part)
    drrecv[rows_at(col)] = drsend[rows_at(col)]

    db = min(256, width)

    def grad_in_w(i, c):
        ds = pl.ds(pl.multiple_of(i * db, db), db)
        wi[ds, :] = dot(recv_t[:, ds], hgr[...], ((0,), (0,))).astype(BF)
        pltpu.make_async_copy(wi.at[ds], dwi_hbm.at[0, ds], osem.at[0]).start()
        return c
    lax.fori_loop(0, width // db, grad_in_w, 0)

    others = pl.ds(0, n - n_row)
    wait_rows(rwrecv, others, small_sem.at[3])
    for e in range(n):
        rwmat[e:e + 1, :] = rwrecv[(e % n_col) * n_row + e // n_col]
    router_part = dot(lg, rwmat[...].astype(BF), ((0,), (0,)))

    wait_rows(drrecv, others, small_sem.at[2])
    total = drrecv[0:n_row]
    for c in range(1, n_col):
        total = total + drrecv[c * n_row:(c + 1) * n_row]
    drsum[...] = total
    for k in range(1, n_row):
        r = lax.rem(row + k, n_row)
        push(drsum.at[r], drz.at[row], ssem.at[7], small_sem.at[4], (r, col))
    drz[pl.ds(row, 1)] = drsum[pl.ds(row, 1)]

    def grad_out_w(i, c):
        fs = pl.ds(pl.multiple_of(i * fb, fb), fb)
        wo[fs, :] = dot(hid[:, fs], recv_s[...], ((0,), (0,))).astype(BF)
        pltpu.make_async_copy(wo.at[fs], dwo_hbm.at[0, fs], osem.at[1]).start()
        return c
    lax.fori_loop(0, ffn // fb, grad_out_w, 0)

    at = lax.broadcasted_iota(jnp.int32, (tok, n * cap), 1).astype(F32)
    pick = (at == upright(slot)).astype(F32).astype(BF)
    for dz in turns:
        wait_rows(gback, chunk_of(xor_row(row, dz)), rg_sem.at[dz])
    dtok_ref[...] = (dot(pick, gback[...]) + router_part).astype(BF)

    wait_rows(drz, pl.ds(0, n_row - 1), small_sem.at[4])
    drouter_ref[...] = jnp.sum(drz[...], axis=0)

    most = pl.ds(0, (n - 1) * cap)
    wait_rows(send_t, most, ssem.at[0])
    wait_rows(send_s, most, ssem.at[1])
    wait_rows(gout, most, ssem.at[2])
    wait_rows(rwrecv, pl.ds(0, n_row - 1), ssem.at[3])
    wait_rows(screcv, pl.ds(0, n - 1), ssem.at[4])
    wait_rows(drsend, others, ssem.at[5])
    wait_rows(rwrecv, others, ssem.at[6])
    wait_rows(drsum, pl.ds(0, n_row - 1), ssem.at[7])
    pltpu.make_async_copy(wi, dwi_hbm.at[0], osem.at[0]).wait()
    pltpu.make_async_copy(wo, dwo_hbm.at[0], osem.at[1]).wait()


def hand_over(dtok, drouter, dwi, dwo, dtok_out, drouter_out, dwi_out, dwo_out):
    dtok_out[...] = dtok[...]
    drouter_out[...] = drouter[...]
    dwi_out[...] = dwi[...]
    dwo_out[...] = dwo[...]


def per_device(tokens, out_grad, expert_ids, router_logits, router_weight, w_in, w_out):
    n_row = lax.axis_size("row")
    n_col = lax.axis_size("col")
    n = n_row * n_col
    tok, width = tokens.shape
    ffn = w_in.shape[2]
    cap = max(16, 2 * tok // n)
    rows = n * cap
    crows = n_col * cap
    vm = pl.BlockSpec(memory_space=pltpu.VMEM)
    hbm = pl.BlockSpec(memory_space=pl.ANY)
    dma = pltpu.SemaphoreType.DMA
    big = pltpu.VMEM((rows, width), BF)
    line = pltpu.VMEM((n, 1, width), F32)
    few = pltpu.VMEM((n_row, 1, width), F32)
    limit = 60 * 1024 * 1024
    shape = jax.ShapeDtypeStruct
    shapes = (
        shape((tok, width), BF),
        shape((1, width), F32),
        shape(w_in.shape, BF),
        shape(w_out.shape, BF),
    )
    results = pl.pallas_call(
        functools.partial(kernel, n_row, n_col, cap, min(512, ffn)),
        out_shape=shapes,
        in_specs=[vm] * 5 + [hbm] * 2,
        out_specs=(vm, vm, hbm, hbm),
        scratch_shapes=[
            pltpu.VMEM((width, ffn), BF),
            pltpu.VMEM((ffn, width), BF),
            big, big, big, big, big, big,
            pltpu.VMEM((rows, ffn), BF),
            pltpu.VMEM((rows, ffn), BF),
            pltpu.VMEM((crows, width), F32),
            line,
            pltpu.VMEM((n, width), F32),
            pltpu.VMEM((n_row, 1, crows), F32),
            pltpu.VMEM((n, 1, crows), F32),
            pltpu.VMEM((n, crows), F32),
            line, line, few, few,
            dma((2,)),
            dma((2,)),
            dma((8,)),
            dma((n_row,)),
            dma((n_row,)),
            dma((n_row,)),
            dma((5,)),
        ],
        compiler_params=pltpu.CompilerParams(
            collective_id=0, has_side_effects=True, vmem_limit_bytes=limit
        ),
        cost_estimate=pl.CostEstimate(
            flops=10 * rows * width * ffn, bytes_accessed=8 * width * ffn, transcendentals=0
        ),
    )(tokens, out_grad, expert_ids[None, :], router_logits.T, router_weight, w_in, w_out)

    steps = 8
    blocks = (
        pl.BlockSpec((tok // steps, width), lambda i: (i, 0)),
        pl.BlockSpec((1, width), lambda i: (0, 0)),
        pl.BlockSpec((1, width // steps, ffn), lambda i: (0, i, 0)),
        pl.BlockSpec((1, ffn // steps, width), lambda i: (0, i, 0)),
    )
    d_tokens, d_router, d_wi, d_wo = pl.pallas_call(
        hand_over,
        grid=(steps,),
        out_shape=shapes,
        in_specs=blocks,
        out_specs=blocks,
        compiler_params=pltpu.CompilerParams(vmem_limit_bytes=limit),
        cost_estimate=pl.CostEstimate(
            flops=0, bytes_accessed=8 * width * ffn, transcendentals=0
        ),
    )(*results)
    return d_tokens, d_wi, d_wo, d_router


def solution(mesh):
    both = ("row", "col")
    flat, cube = P(both, None), P(both, None, None)
    return jax.shard_map(
        per_device,
        mesh=mesh,
        in_specs=(flat, flat, P(both), flat, flat, cube, cube),
        out_specs=(flat, cube, cube, flat),
        check_vma=False,
    )
```

```python
import functools

import jax
import jax.numpy as jnp
from jax import lax
from jax.experimental import pallas as pl
from jax.experimental.pallas import tpu as pltpu
from jax.sharding import PartitionSpec as P

MESH = pl.DeviceIdType.MESH
BF = jnp.bfloat16
F32 = jnp.float32


def dot(a, b, dims=((1,), (0,)), **kw):
    return lax.dot_general(a, b, (dims, ((), ())), preferred_element_type=F32, **kw)


def xor_row(row, dz):
    out, bit = 0, 1
    while bit < 8:
        out = out + bit * (((row // bit) % 2 + (dz // bit) % 2) % 2)
        bit *= 2
    return out


def kernel(
    n_row, n_col, cap, fb,
    tok_ref, og_ref, ids_ref, logit_ref, rw_ref, wi_hbm, wo_hbm,
    dtok_ref, drouter_ref, dwi_hbm, dwo_hbm,
    wi, wo, send_t, send_s, recv_t, recv_s, gout, gback, hid, hgr, acc,
    rwrecv, rwmat, scsend, screcv, scmat, drsend, drrecv, drsum, drz,
    wsem, osem, ssem, rt_sem, rs_sem, rg_sem, small_sem,
):
    n = n_row * n_col
    row = lax.axis_index("row")
    col = lax.axis_index("col")
    me = row * n_col + col
    tok, width = tok_ref.shape
    ffn = wi.shape[1]
    crows = n_col * cap

    def rows_of(dev):
        return pl.ds(pl.multiple_of(dev * cap, cap), cap)

    def chunk_of(r):
        return pl.ds(pl.multiple_of(r * crows, crows), crows)

    def rows_at(c):
        return pl.ds(c * n_row, n_row)

    load_i = pltpu.make_async_copy(wi_hbm.at[0], wi, wsem.at[0])
    load_o = pltpu.make_async_copy(wo_hbm.at[0], wo, wsem.at[1])
    load_i.start()
    load_o.start()

    barrier = pltpu.get_barrier_semaphore()

    def greet(k, c):
        peer = lax.rem(me + k, n)
        pl.semaphore_signal(
            barrier, inc=1, device_id=(peer // n_col, lax.rem(peer, n_col)),
            device_id_type=MESH)
        return c
    lax.fori_loop(1, n, greet, 0)

    ids = ids_ref[...]
    chosen = (ids == lax.broadcasted_iota(jnp.int32, (n, tok), 0)).astype(F32)
    it0 = lax.broadcasted_iota(jnp.int32, (tok, tok), 0)
    it1 = lax.broadcasted_iota(jnp.int32, (tok, tok), 1)
    earlier = dot(chosen.astype(BF), (it0 < it1).astype(F32).astype(BF))
    rank = jnp.sum(earlier * chosen, axis=0, keepdims=True)
    slot = ids.astype(F32) * cap + rank
    tokens = tok_ref[...]

    def upright(x):
        return jnp.sum(jnp.where(it0 == it1, x, 0.0), axis=1, keepdims=True)

    def fill(ref, values, dz):
        r = xor_row(row, dz)
        at = lax.broadcasted_iota(jnp.int32, (crows, tok), 0).astype(F32) + (
            r * crows).astype(F32)
        pick = (at == slot).astype(F32).astype(BF)
        ref[chunk_of(r), :] = dot(pick, values).astype(BF)

    def push(src, dst, sem, rsem, dev):
        pltpu.make_async_remote_copy(
            src_ref=src, dst_ref=dst, send_sem=sem, recv_sem=rsem,
            device_id=dev, device_id_type=MESH,
        ).start()

    def col_loop(first, last, body):
        def step(j, c):
            body(lax.rem(col + j, n_col))
            return c
        lax.fori_loop(first, last, step, 0)

    def send_tokens(dz, c):
        r = xor_row(row, dz)
        push(send_t.at[rows_of(r * n_col + c)], recv_t.at[rows_of(me)],
             ssem.at[0], rt_sem.at[dz], (r, c))

    def send_scaled(dz, c):
        r = xor_row(row, dz)
        push(send_s.at[rows_of(r * n_col + c)], recv_s.at[rows_of(me)],
             ssem.at[1], rs_sem.at[dz], (r, c))

    def dispatch(far, near, sends):
        for send in sends:
            send(far, col)
            if near:
                send(near, col)

        def both(c):
            for send in sends:
                send(far, c)
                send(near, c)
        col_loop(1, n_col, both)

    half = n_row // 2
    fill(send_t, tokens, half)
    fill(send_t, tokens, 0)
    pl.semaphore_wait(barrier, n - 1)

    mine = col * n_row + row
    rwrecv[pl.ds(mine, 1)] = rw_ref[...].astype(F32)[None]
    for k in range(1, n_row):
        push(rwrecv.at[mine], rwrecv.at[mine], ssem.at[3], small_sem.at[0],
             (lax.rem(row + k, n_row), col))

    dispatch(half, 0, (send_tokens,))
    pltpu.make_async_copy(
        send_t.at[rows_of(me)], recv_t.at[rows_of(me)], rt_sem.at[0]).start()

    logits = logit_ref[...]
    ex = jnp.exp(logits - jnp.max(logits, axis=0, keepdims=True))
    probs = ex / jnp.sum(ex, axis=0, keepdims=True)
    gate = jnp.sum(probs * chosen, axis=0, keepdims=True)
    scaled = (upright(gate) * og_ref[...].astype(F32)).astype(BF)
    fill(send_s, scaled, half)
    fill(send_s, scaled, 0)
    dispatch(half, 0, (send_scaled,))
    pltpu.make_async_copy(
        send_s.at[rows_of(me)], recv_s.at[rows_of(me)], rs_sem.at[0]).start()
    for near in range(1, half):
        for dz in (half + near, near):
            fill(send_t, tokens, dz)
            fill(send_s, scaled, dz)
        dispatch(half + near, near, (send_tokens, send_scaled))

    def wait_rows(ref, sl, sem):
        pltpu.make_async_copy(ref.at[sl], ref.at[sl], sem).wait()

    load_i.wait()
    load_o.wait()
    eye = (lax.broadcasted_iota(jnp.int32, (crows, crows), 0)
           == lax.broadcasted_iota(jnp.int32, (crows, crows), 1))

    def give(dz, first, last):
        r = xor_row(row, dz)

        def send(c):
            push(gout.at[rows_of(r * n_col + c)], gback.at[rows_of(me)],
                 ssem.at[2], rg_sem.at[dz], (r, c))
        col_loop(first, last, send)

    turns = [dz for near in range(half) for dz in (near, half + near)]
    for dz in turns:
        r = xor_row(row, dz)
        sl = chunk_of(r)
        wait_rows(recv_t, sl, rt_sem.at[dz])
        wait_rows(recv_s, sl, rs_sem.at[dz])
        acc[...] = jnp.zeros_like(acc)

        def block(f, v, sl=sl):
            fs = pl.ds(pl.multiple_of(f * fb, fb), fb)
            w1 = wi[:, fs]
            pre = dot(recv_t[sl, :], w1)
            back = dot(recv_s[sl, :], wo[fs, :], ((1,), (1,)))
            h = jnp.maximum(pre, 0.0).astype(BF)
            g = jnp.where(pre > 0.0, back, 0.0).astype(BF)
            hid[sl, fs] = h
            hgr[sl, fs] = g
            acc[...] += dot(g, w1, ((1,), (1,)))
            return v + jnp.sum(h.astype(F32) * back, axis=1, keepdims=True)

        v = lax.fori_loop(0, ffn // fb, block, jnp.zeros((crows, 1), F32))
        gout[sl, :] = acc[...].astype(BF)
        scsend[pl.ds(r, 1)] = jnp.sum(
            jnp.where(eye, v, 0.0), axis=0, keepdims=True)[None]

        def tell(c, r=r):
            push(scsend.at[r], screcv.at[me], ssem.at[4], small_sem.at[1], (r, c))
        if dz == 0:
            pltpu.make_async_copy(
                gout.at[rows_of(me)], gback.at[rows_of(me)], rg_sem.at[0]).start()
            pltpu.make_async_copy(scsend.at[r], screcv.at[me], small_sem.at[1]).start()
        col_loop(0 if dz else 1, n_col, tell)
        give(dz, 0 if dz else 1, n_col)
        if dz == half:
            wait_rows(rwrecv, pl.ds(0, n_row - 1), small_sem.at[0])

            def pass_on(c):
                push(rwrecv.at[rows_at(col)], rwrecv.at[rows_at(col)],
                     ssem.at[6], small_sem.at[3], (row, c))
            col_loop(1, n_col, pass_on)

    pltpu.make_async_copy(screcv, screcv, small_sem.at[1]).wait()
    for e in range(n):
        scmat[e:e + 1, :] = screcv[e]
    picked = dot(scmat[...], chosen, ((0,), (0,)), precision=lax.Precision.HIGHEST)
    lane = lax.broadcasted_iota(jnp.int32, (crows, tok), 0).astype(F32)
    own = (col * cap).astype(F32) + rank
    vg = jnp.sum(jnp.where(lane == own, picked, 0.0), axis=0, keepdims=True)
    lg = (vg * (chosen - probs)).astype(BF)
    part = dot(lg, tokens)
    for e in range(n):
        drsend[(e % n_col) * n_row + e // n_col] = part[e:e + 1, :]

    def gather_part(c):
        push(drsend.at[rows_at(c)], drrecv.at[rows_at(col)],
             ssem.at[5], small_sem.at[2], (row, c))
    col_loop(1, n_col, gather_part)
    drrecv[rows_at(col)] = drsend[rows_at(col)]

    db = min(256, width)

    def grad_in_w(i, c):
        ds = pl.ds(pl.multiple_of(i * db, db), db)
        wi[ds, :] = dot(recv_t[:, ds], hgr[...], ((0,), (0,))).astype(BF)
        pltpu.make_async_copy(wi.at[ds], dwi_hbm.at[0, ds], osem.at[0]).start()
        return c
    lax.fori_loop(0, width // db, grad_in_w, 0)

    others = pl.ds(0, n - n_row)
    wait_rows(rwrecv, others, small_sem.at[3])
    for e in range(n):
        rwmat[e:e + 1, :] = rwrecv[(e % n_col) * n_row + e // n_col]
    router_part = dot(lg, rwmat[...].astype(BF), ((0,), (0,)))

    wait_rows(drrecv, others, small_sem.at[2])
    total = drrecv[0:n_row]
    for c in range(1, n_col):
        total = total + drrecv[c * n_row:(c + 1) * n_row]
    drsum[...] = total
    for k in range(1, n_row):
        r = lax.rem(row + k, n_row)
        push(drsum.at[r], drz.at[row], ssem.at[7], small_sem.at[4], (r, col))
    drz[pl.ds(row, 1)] = drsum[pl.ds(row, 1)]

    def grad_out_w(i, c):
        fs = pl.ds(pl.multiple_of(i * fb, fb), fb)
        wo[fs, :] = dot(hid[:, fs], recv_s[...], ((0,), (0,))).astype(BF)
        pltpu.make_async_copy(wo.at[fs], dwo_hbm.at[0, fs], osem.at[1]).start()
        return c
    lax.fori_loop(0, ffn // fb, grad_out_w, 0)

    at = lax.broadcasted_iota(jnp.int32, (tok, n * cap), 1).astype(F32)
    pick = (at == upright(slot)).astype(F32).astype(BF)
    for dz in turns:
        wait_rows(gback, chunk_of(xor_row(row, dz)), rg_sem.at[dz])
    dtok_ref[...] = (dot(pick, gback[...]) + router_part).astype(BF)

    wait_rows(drz, pl.ds(0, n_row - 1), small_sem.at[4])
    drouter_ref[...] = jnp.sum(drz[...], axis=0)

    most = pl.ds(0, (n - 1) * cap)
    wait_rows(send_t, most, ssem.at[0])
    wait_rows(send_s, most, ssem.at[1])
    wait_rows(gout, most, ssem.at[2])
    wait_rows(rwrecv, pl.ds(0, n_row - 1), ssem.at[3])
    wait_rows(screcv, pl.ds(0, n - 1), ssem.at[4])
    wait_rows(drsend, others, ssem.at[5])
    wait_rows(rwrecv, others, ssem.at[6])
    wait_rows(drsum, pl.ds(0, n_row - 1), ssem.at[7])
    pltpu.make_async_copy(wi, dwi_hbm.at[0], osem.at[0]).wait()
    pltpu.make_async_copy(wo, dwo_hbm.at[0], osem.at[1]).wait()


def hand_over(parts, dtok, drouter, dwi, dwo, dtok_out, drouter_out, dwi_out, dwo_out, sem):
    copies = [(dtok, dtok_out), (drouter, drouter_out)]
    for src, dst in ((dwi, dwi_out), (dwo, dwo_out)):
        step = src.shape[1] // parts
        for i in range(parts):
            at = pl.ds(i * step, step)
            copies.append((src.at[0, at], dst.at[0, at]))
    copies = [pltpu.make_async_copy(*pair, sem.at[i]) for i, pair in enumerate(copies)]
    for copy in copies:
        copy.start()
    for copy in copies:
        copy.wait()


def per_device(tokens, out_grad, expert_ids, router_logits, router_weight, w_in, w_out):
    n_row = lax.axis_size("row")
    n_col = lax.axis_size("col")
    n = n_row * n_col
    tok, width = tokens.shape
    ffn = w_in.shape[2]
    cap = max(16, 2 * tok // n)
    rows = n * cap
    crows = n_col * cap
    vm = pl.BlockSpec(memory_space=pltpu.VMEM)
    hbm = pl.BlockSpec(memory_space=pl.ANY)
    dma = pltpu.SemaphoreType.DMA
    big = pltpu.VMEM((rows, width), BF)
    line = pltpu.VMEM((n, 1, width), F32)
    few = pltpu.VMEM((n_row, 1, width), F32)
    held = 4 * width * ffn + 2 * rows * (6 * width + 2 * ffn) + 4 * crows * width
    limit = held + 9 * 1024 * 1024
    shape = jax.ShapeDtypeStruct
    shapes = (
        shape((tok, width), BF),
        shape((1, width), F32),
        shape(w_in.shape, BF),
        shape(w_out.shape, BF),
    )
    results = pl.pallas_call(
        functools.partial(kernel, n_row, n_col, cap, min(512, ffn)),
        out_shape=shapes,
        in_specs=[vm] * 5 + [pl.BlockSpec(memory_space=pltpu.HBM)] * 2,
        out_specs=(vm, vm, hbm, hbm),
        scratch_shapes=[
            pltpu.VMEM((width, ffn), BF),
            pltpu.VMEM((ffn, width), BF),
            big, big, big, big, big, big,
            pltpu.VMEM((rows, ffn), BF),
            pltpu.VMEM((rows, ffn), BF),
            pltpu.VMEM((crows, width), F32),
            line,
            pltpu.VMEM((n, width), F32),
            pltpu.VMEM((n_row, 1, crows), F32),
            pltpu.VMEM((n, 1, crows), F32),
            pltpu.VMEM((n, crows), F32),
            line, line, few, few,
            dma((2,)),
            dma((2,)),
            dma((8,)),
            dma((n_row,)),
            dma((n_row,)),
            dma((n_row,)),
            dma((5,)),
        ],
        compiler_params=pltpu.CompilerParams(
            collective_id=0, has_side_effects=True, vmem_limit_bytes=limit
        ),
        cost_estimate=pl.CostEstimate(
            flops=10 * rows * width * ffn, bytes_accessed=8 * width * ffn, transcendentals=0
        ),
    )(tokens, out_grad, expert_ids[None, :], router_logits.T, router_weight,
      pltpu.with_memory_space_constraint(w_in, pltpu.HBM),
      pltpu.with_memory_space_constraint(w_out, pltpu.HBM))

    parts = 4
    d_tokens, d_router, d_wi, d_wo = pl.pallas_call(
        functools.partial(hand_over, parts),
        out_shape=shapes,
        in_specs=[hbm] * 4,
        out_specs=[hbm] * 4,
        scratch_shapes=[dma((2 + 2 * parts,))],
        compiler_params=pltpu.CompilerParams(vmem_limit_bytes=4 * 1024 * 1024),
        cost_estimate=pl.CostEstimate(
            flops=0, bytes_accessed=4 * width * ffn, transcendentals=0
        ),
    )(*results)
    return d_tokens, d_wi, d_wo, d_router


def solution(mesh):
    both = ("row", "col")
    flat, cube = P(both, None), P(both, None, None)
    return jax.shard_map(
        per_device,
        mesh=mesh,
        in_specs=(flat, flat, P(both), flat, flat, cube, cube),
        out_specs=(flat, cube, cube, flat),
        check_vma=False,
    )
```

```python
import functools

import jax
import jax.numpy as jnp
from jax import lax
from jax.experimental import pallas as pl
from jax.experimental.pallas import tpu as pltpu
from jax.sharding import PartitionSpec as P

MESH = pl.DeviceIdType.MESH
BF = jnp.bfloat16
F32 = jnp.float32


def dot(a, b, dims=((1,), (0,)), **kw):
    return lax.dot_general(a, b, (dims, ((), ())), preferred_element_type=F32, **kw)


def xor_row(row, dz):
    out, bit = 0, 1
    while bit < 8:
        out = out + bit * (((row // bit) % 2 + (dz // bit) % 2) % 2)
        bit *= 2
    return out


def kernel(
    n_row, n_col, cap, fb,
    tok_ref, og_ref, ids_ref, logit_ref, rw_ref, wi_hbm, wo_hbm,
    dtok_ref, drouter_ref, dwi_hbm, dwo_hbm,
    wi, wo, send_t, send_s, recv_t, recv_s, gout, gback, hid, hgr, acc,
    rwrecv, rwmat, scsend, screcv, scmat, drsend, drrecv, drsum, drz,
    wsem, osem, ssem, rt_sem, rs_sem, rg_sem, small_sem,
):
    n = n_row * n_col
    row = lax.axis_index("row")
    col = lax.axis_index("col")
    me = row * n_col + col
    tok, width = tok_ref.shape
    ffn = wi.shape[1]
    crows = n_col * cap

    def rows_of(dev):
        return pl.ds(pl.multiple_of(dev * cap, cap), cap)

    def chunk_of(r):
        return pl.ds(pl.multiple_of(r * crows, crows), crows)

    def rows_at(c):
        return pl.ds(c * n_row, n_row)

    load_i = pltpu.make_async_copy(wi_hbm.at[0], wi, wsem.at[0])
    load_o = pltpu.make_async_copy(wo_hbm.at[0], wo, wsem.at[1])
    load_i.start()
    load_o.start()

    barrier = pltpu.get_barrier_semaphore()

    def greet(k, c):
        peer = lax.rem(me + k, n)
        pl.semaphore_signal(
            barrier, inc=1, device_id=(peer // n_col, lax.rem(peer, n_col)),
            device_id_type=MESH)
        return c
    lax.fori_loop(1, n, greet, 0)

    ids = ids_ref[...]
    chosen = (ids == lax.broadcasted_iota(jnp.int32, (n, tok), 0)).astype(F32)
    it0 = lax.broadcasted_iota(jnp.int32, (tok, tok), 0)
    it1 = lax.broadcasted_iota(jnp.int32, (tok, tok), 1)
    earlier = dot(chosen.astype(BF), (it0 < it1).astype(F32).astype(BF))
    rank = jnp.sum(earlier * chosen, axis=0, keepdims=True)
    slot = ids.astype(F32) * cap + rank
    tokens = tok_ref[...]

    def upright(x):
        return jnp.sum(jnp.where(it0 == it1, x, 0.0), axis=1, keepdims=True)

    def fill(ref, values, dz):
        r = xor_row(row, dz)
        at = lax.broadcasted_iota(jnp.int32, (crows, tok), 0).astype(F32) + (
            r * crows).astype(F32)
        pick = (at == slot).astype(F32).astype(BF)
        ref[chunk_of(r), :] = dot(pick, values).astype(BF)

    def push(src, dst, sem, rsem, dev):
        pltpu.make_async_remote_copy(
            src_ref=src, dst_ref=dst, send_sem=sem, recv_sem=rsem,
            device_id=dev, device_id_type=MESH,
        ).start()

    def col_loop(first, last, body):
        def step(j, c):
            body(lax.rem(col + j, n_col))
            return c
        lax.fori_loop(first, last, step, 0)

    def send_tokens(dz, c):
        r = xor_row(row, dz)
        push(send_t.at[rows_of(r * n_col + c)], recv_t.at[rows_of(me)],
             ssem.at[0], rt_sem.at[dz], (r, c))

    def send_scaled(dz, c):
        r = xor_row(row, dz)
        push(send_s.at[rows_of(r * n_col + c)], recv_s.at[rows_of(me)],
             ssem.at[1], rs_sem.at[dz], (r, c))

    def dispatch(far, near, sends):
        for send in sends:
            send(far, col)
            if near:
                send(near, col)

        def both(c):
            for send in sends:
                send(far, c)
                send(near, c)
        col_loop(1, n_col, both)

    half = n_row // 2
    fill(send_t, tokens, half)
    fill(send_t, tokens, 0)
    pl.semaphore_wait(barrier, n - 1)

    mine = col * n_row + row
    rwrecv[pl.ds(mine, 1)] = rw_ref[...].astype(F32)[None]
    for k in range(1, n_row):
        push(rwrecv.at[mine], rwrecv.at[mine], ssem.at[3], small_sem.at[0],
             (lax.rem(row + k, n_row), col))

    dispatch(half, 0, (send_tokens,))
    pltpu.make_async_copy(
        send_t.at[rows_of(me)], recv_t.at[rows_of(me)], rt_sem.at[0]).start()

    logits = logit_ref[...]
    ex = jnp.exp(logits - jnp.max(logits, axis=0, keepdims=True))
    probs = ex / jnp.sum(ex, axis=0, keepdims=True)
    gate = jnp.sum(probs * chosen, axis=0, keepdims=True)
    scaled = (upright(gate) * og_ref[...].astype(F32)).astype(BF)
    fill(send_s, scaled, half)
    fill(send_s, scaled, 0)
    dispatch(half, 0, (send_scaled,))
    pltpu.make_async_copy(
        send_s.at[rows_of(me)], recv_s.at[rows_of(me)], rs_sem.at[0]).start()
    for near in range(1, half):
        for dz in (half + near, near):
            fill(send_t, tokens, dz)
            fill(send_s, scaled, dz)
        dispatch(half + near, near, (send_tokens, send_scaled))

    def wait_rows(ref, sl, sem):
        pltpu.make_async_copy(ref.at[sl], ref.at[sl], sem).wait()

    load_i.wait()
    load_o.wait()
    eye = (lax.broadcasted_iota(jnp.int32, (crows, crows), 0)
           == lax.broadcasted_iota(jnp.int32, (crows, crows), 1))

    def give(dz, first, last):
        r = xor_row(row, dz)

        def send(c):
            push(gout.at[rows_of(r * n_col + c)], gback.at[rows_of(me)],
                 ssem.at[2], rg_sem.at[dz], (r, c))
        col_loop(first, last, send)

    turns = [dz for near in range(half) for dz in (near, half + near)]
    for dz in turns:
        r = xor_row(row, dz)
        sl = chunk_of(r)
        wait_rows(recv_t, sl, rt_sem.at[dz])
        wait_rows(recv_s, sl, rs_sem.at[dz])
        acc[...] = jnp.zeros_like(acc)

        def block(f, v, sl=sl):
            fs = pl.ds(pl.multiple_of(f * fb, fb), fb)
            w1 = wi[:, fs]
            pre = dot(recv_t[sl, :], w1)
            back = dot(recv_s[sl, :], wo[fs, :], ((1,), (1,)))
            h = jnp.maximum(pre, 0.0).astype(BF)
            g = jnp.where(pre > 0.0, back, 0.0).astype(BF)
            hid[sl, fs] = h
            hgr[sl, fs] = g
            acc[...] += dot(g, w1, ((1,), (1,)))
            return v + jnp.sum(h.astype(F32) * back, axis=1, keepdims=True)

        v = lax.fori_loop(0, ffn // fb, block, jnp.zeros((crows, 1), F32))
        gout[sl, :] = acc[...].astype(BF)
        scsend[pl.ds(r, 1)] = jnp.sum(
            jnp.where(eye, v, 0.0), axis=0, keepdims=True)[None]

        def tell(c, r=r):
            push(scsend.at[r], screcv.at[me], ssem.at[4], small_sem.at[1], (r, c))
        if dz == 0:
            pltpu.make_async_copy(
                gout.at[rows_of(me)], gback.at[rows_of(me)], rg_sem.at[0]).start()
            pltpu.make_async_copy(scsend.at[r], screcv.at[me], small_sem.at[1]).start()
        col_loop(0 if dz else 1, n_col, tell)
        give(dz, 0 if dz else 1, n_col)
        if dz == half:
            wait_rows(rwrecv, pl.ds(0, n_row - 1), small_sem.at[0])

            def pass_on(c):
                push(rwrecv.at[rows_at(col)], rwrecv.at[rows_at(col)],
                     ssem.at[6], small_sem.at[3], (row, c))
            col_loop(1, n_col, pass_on)

    pltpu.make_async_copy(screcv, screcv, small_sem.at[1]).wait()
    for e in range(n):
        scmat[e:e + 1, :] = screcv[e]
    picked = dot(scmat[...], chosen, ((0,), (0,)), precision=lax.Precision.HIGHEST)
    lane = lax.broadcasted_iota(jnp.int32, (crows, tok), 0).astype(F32)
    own = (col * cap).astype(F32) + rank
    vg = jnp.sum(jnp.where(lane == own, picked, 0.0), axis=0, keepdims=True)
    lg = (vg * (chosen - probs)).astype(BF)
    part = dot(lg, tokens)
    for e in range(n):
        drsend[(e % n_col) * n_row + e // n_col] = part[e:e + 1, :]

    def gather_part(c):
        push(drsend.at[rows_at(c)], drrecv.at[rows_at(col)],
             ssem.at[5], small_sem.at[2], (row, c))
    col_loop(1, n_col, gather_part)
    drrecv[rows_at(col)] = drsend[rows_at(col)]

    db = min(256, width)

    def grad_in_w(i, c):
        ds = pl.ds(pl.multiple_of(i * db, db), db)
        wi[ds, :] = dot(recv_t[:, ds], hgr[...], ((0,), (0,))).astype(BF)
        pltpu.make_async_copy(wi.at[ds], dwi_hbm.at[0, ds], osem.at[0]).start()
        return c
    lax.fori_loop(0, width // db, grad_in_w, 0)

    others = pl.ds(0, n - n_row)
    wait_rows(rwrecv, others, small_sem.at[3])
    for e in range(n):
        rwmat[e:e + 1, :] = rwrecv[(e % n_col) * n_row + e // n_col]
    router_part = dot(lg, rwmat[...].astype(BF), ((0,), (0,)))

    wait_rows(drrecv, others, small_sem.at[2])
    total = drrecv[0:n_row]
    for c in range(1, n_col):
        total = total + drrecv[c * n_row:(c + 1) * n_row]
    drsum[...] = total
    for k in range(1, n_row):
        r = lax.rem(row + k, n_row)
        push(drsum.at[r], drz.at[row], ssem.at[7], small_sem.at[4], (r, col))
    drz[pl.ds(row, 1)] = drsum[pl.ds(row, 1)]

    def grad_out_w(i, c):
        fs = pl.ds(pl.multiple_of(i * fb, fb), fb)
        wo[fs, :] = dot(hid[:, fs], recv_s[...], ((0,), (0,))).astype(BF)
        pltpu.make_async_copy(wo.at[fs], dwo_hbm.at[0, fs], osem.at[1]).start()
        return c
    lax.fori_loop(0, ffn // fb, grad_out_w, 0)

    at = lax.broadcasted_iota(jnp.int32, (tok, n * cap), 1).astype(F32)
    pick = (at == upright(slot)).astype(F32).astype(BF)
    for dz in turns:
        wait_rows(gback, chunk_of(xor_row(row, dz)), rg_sem.at[dz])
    dtok_ref[...] = (dot(pick, gback[...]) + router_part).astype(BF)

    wait_rows(drz, pl.ds(0, n_row - 1), small_sem.at[4])
    drouter_ref[...] = jnp.sum(drz[...], axis=0)

    most = pl.ds(0, (n - 1) * cap)
    wait_rows(send_t, most, ssem.at[0])
    wait_rows(send_s, most, ssem.at[1])
    wait_rows(gout, most, ssem.at[2])
    wait_rows(rwrecv, pl.ds(0, n_row - 1), ssem.at[3])
    wait_rows(screcv, pl.ds(0, n - 1), ssem.at[4])
    wait_rows(drsend, others, ssem.at[5])
    wait_rows(rwrecv, others, ssem.at[6])
    wait_rows(drsum, pl.ds(0, n_row - 1), ssem.at[7])
    pltpu.make_async_copy(wi, dwi_hbm.at[0], osem.at[0]).wait()
    pltpu.make_async_copy(wo, dwo_hbm.at[0], osem.at[1]).wait()


def hand_over(parts, dtok, drouter, dwi, dwo, dtok_out, drouter_out, dwi_out, dwo_out, sem):
    copies = [(dtok, dtok_out), (drouter, drouter_out)]
    for src, dst in ((dwi, dwi_out), (dwo, dwo_out)):
        step = src.shape[1] // parts
        for i in range(parts):
            at = pl.ds(i * step, step)
            copies.append((src.at[0, at], dst.at[0, at]))
    copies = [pltpu.make_async_copy(*pair, sem.at[i]) for i, pair in enumerate(copies)]
    for copy in copies:
        copy.start()
    for copy in copies:
        copy.wait()


def per_device(tokens, out_grad, expert_ids, router_logits, router_weight, w_in, w_out):
    n_row = lax.axis_size("row")
    n_col = lax.axis_size("col")
    n = n_row * n_col
    tok, width = tokens.shape
    ffn = w_in.shape[2]
    cap = max(16, 2 * tok // n)
    rows = n * cap
    crows = n_col * cap
    vm = pl.BlockSpec(memory_space=pltpu.VMEM)
    hbm = pl.BlockSpec(memory_space=pl.ANY)
    dma = pltpu.SemaphoreType.DMA
    big = pltpu.VMEM((rows, width), BF)
    line = pltpu.VMEM((n, 1, width), F32)
    few = pltpu.VMEM((n_row, 1, width), F32)
    held = 4 * width * ffn + 2 * rows * (6 * width + 2 * ffn) + 4 * crows * width
    limit = held + 9 * 1024 * 1024
    shape = jax.ShapeDtypeStruct
    shapes = (
        shape((tok, width), BF),
        shape((1, width), F32),
        shape(w_in.shape, BF),
        shape(w_out.shape, BF),
    )
    results = pl.pallas_call(
        functools.partial(kernel, n_row, n_col, cap, min(512, ffn)),
        out_shape=shapes,
        in_specs=[vm] * 5 + [pl.BlockSpec(memory_space=pltpu.HBM)] * 2,
        out_specs=(vm, vm, hbm, hbm),
        scratch_shapes=[
            pltpu.VMEM((width, ffn), BF),
            pltpu.VMEM((ffn, width), BF),
            big, big, big, big, big, big,
            pltpu.VMEM((rows, ffn), BF),
            pltpu.VMEM((rows, ffn), BF),
            pltpu.VMEM((crows, width), F32),
            line,
            pltpu.VMEM((n, width), F32),
            pltpu.VMEM((n_row, 1, crows), F32),
            pltpu.VMEM((n, 1, crows), F32),
            pltpu.VMEM((n, crows), F32),
            line, line, few, few,
            dma((2,)),
            dma((2,)),
            dma((8,)),
            dma((n_row,)),
            dma((n_row,)),
            dma((n_row,)),
            dma((5,)),
        ],
        compiler_params=pltpu.CompilerParams(
            collective_id=0, has_side_effects=True, vmem_limit_bytes=limit
        ),
        cost_estimate=pl.CostEstimate(
            flops=10 * rows * width * ffn, bytes_accessed=8 * width * ffn, transcendentals=0
        ),
    )(*(pltpu.with_memory_space_constraint(x, pltpu.HBM) for x in (
        tokens, out_grad, expert_ids[None, :], router_logits.T, router_weight, w_in, w_out)))

    parts = 4
    d_tokens, d_router, d_wi, d_wo = pl.pallas_call(
        functools.partial(hand_over, parts),
        out_shape=shapes,
        in_specs=[hbm] * 4,
        out_specs=[hbm] * 4,
        scratch_shapes=[dma((2 + 2 * parts,))],
        compiler_params=pltpu.CompilerParams(vmem_limit_bytes=4 * 1024 * 1024),
        cost_estimate=pl.CostEstimate(
            flops=0, bytes_accessed=4 * width * ffn, transcendentals=0
        ),
    )(*results)
    return d_tokens, d_wi, d_wo, d_router


def solution(mesh):
    both = ("row", "col")
    flat, cube = P(both, None), P(both, None, None)
    return jax.shard_map(
        per_device,
        mesh=mesh,
        in_specs=(flat, flat, P(both), flat, flat, cube, cube),
        out_specs=(flat, cube, cube, flat),
        check_vma=False,
    )
```
